32 devices in a mesh: ctx: 8 (over z, y), tp: 4 (over x, core).
Axes of the slice: x: 2, y: 2, z: 4, core: 2. Of those that a mesh axis runs over, the one named last changes fastest.
Arguments:
- hidden_in: bfloat16 [4096, 4608], P('ctx'), may hold values from -5.4 to 5.4
- pre_gain: float32 [4608], replicated, may hold values from 0.25 to 1.75
- w_query: bfloat16 [4608, 2048], P(None, 'tp'), may hold values from -0.677644 to 0.677644
- w_key: bfloat16 [4608, 1024], P(None, 'tp'), may hold values from -0.058925565 to 0.058925565
- w_value: bfloat16 [4608, 1024], P(None, 'tp'), may hold values from -0.09375 to 0.09375
- w_out: bfloat16 [2048, 4608], P('tp'), may hold values from -0.26516504 to 0.26516504
- post_gain: float32 [4608], P('tp'), may hold values from 0.25 to 1.75
Outputs:
- layer_out: bfloat16 [4096, 4608], P('ctx', 'tp')
- sink_share: float32 [4096], P('ctx')
The draws below stay inside these ranges and needn't reach their ends.
All inputs are finite; a program needn't handle non-finite values.
Results may differ from the reference program's by a relative error of at most 0.0095.
The reference program's roundings to bfloat16 on the way (of `normed`, `weight16` and `attended`) count: a program that leaves them out, or rounds other values in their place, can miss the bound.
Values may be sent and summed in bfloat16 or wider, within the bound.
A program may use at most 192 MiB of HBM per device.

```python
import jax
import jax.numpy as jnp
from jax import lax

D = 4608
QHEADS = 16
KVHEADS = 8
HEAD = 128
WINDOW = 4096
SINKS = 4
TOKENS = 4096


def draw_hidden_in(key, part):
    first, second, third = jax.random.split(key, 3)
    row_scale = jnp.exp(jax.random.uniform(second, (TOKENS, 1), jnp.float32, jnp.log(jnp.float32(0.03)), jnp.log(jnp.float32(0.3))))
    col_scale = jnp.exp(jax.random.uniform(third, (1, D), jnp.float32, jnp.log(jnp.float32(0.3)), jnp.log(jnp.float32(3.0))))
    base = jnp.clip(jax.random.normal(first, (TOKENS, D), jnp.float32), -6.0, 6.0)
    return (base * row_scale * col_scale).astype(jnp.bfloat16)


def key_columns(key):
    base = jax.random.normal(jax.random.fold_in(key, 101), (D, KVHEADS * HEAD), jnp.float32)
    return jnp.clip(base, -4.0, 4.0) * float(D) ** (-0.5)


def draw_w_key(key, part):
    return key_columns(key).astype(jnp.bfloat16)


def draw_w_query(key, part):
    half = HEAD // 2
    columns = key_columns(key).reshape(D, KVHEADS, HEAD)
    index = jnp.arange(half).astype(jnp.float32) * 2.0
    inverse = jnp.exp(-jnp.log(jnp.float32(10000.0)) * index / HEAD)
    phase = jnp.float32(WINDOW // 2) * inverse
    cosine = jnp.cos(phase)
    sine = jnp.sin(phase)
    first_half = columns[..., :half]
    second_half = columns[..., half:]
    turned = 8.0 * jnp.concatenate([first_half * cosine + second_half * sine, second_half * cosine - first_half * sine], axis=-1)
    turned = jnp.repeat(turned, QHEADS // KVHEADS, axis=1)
    drawn = jnp.clip(jax.random.normal(jax.random.fold_in(key, 102), (D, QHEADS, HEAD), jnp.float32), -4.0, 4.0) * float(D) ** (-0.5)
    order = jax.random.permutation(jax.random.fold_in(key, 103), QHEADS)
    chosen = (order < QHEADS // 4)[None, :, None]
    return jnp.where(chosen, turned, drawn).reshape(D, QHEADS * HEAD).astype(jnp.bfloat16)


def draw_w_out(key, part):
    first = jax.random.fold_in(key, 201)
    second = jax.random.fold_in(key, 202)
    fan_rows = QHEADS * HEAD
    col_scale = jnp.exp(jax.random.uniform(second, (1, D), jnp.float32, jnp.log(jnp.float32(0.3)), jnp.log(jnp.float32(3.0))))
    base = jnp.clip(jax.random.normal(first, (fan_rows, D), jnp.float32), -4.0, 4.0)
    return (base * col_scale * float(fan_rows) ** (-0.5)).astype(jnp.bfloat16)


def block_scale(rng, dims, pieces, least, largest):
    gain, own = 1.0, jax.random.fold_in(rng, 6)
    for axis_at, shards_of in pieces:
        draws = jnp.exp(jax.random.uniform(jax.random.fold_in(own, axis_at), (shards_of,), jnp.float32, least / len(pieces), largest / len(pieces)))
        gain = gain * jnp.repeat(draws, dims[axis_at] // shards_of).reshape([-1 if axis == axis_at else 1 for axis in range(len(dims))])
    return gain


def gaussian(stream_key, shape, spread, most, cuts=(), kind=jnp.bfloat16):
    drawn = jax.random.normal(stream_key, shape, jnp.float32) * spread
    if len(cuts) > 0:
        drawn = block_scale(stream_key, shape, cuts, -0.22, 0.18) * drawn
    return jnp.clip(drawn, min=-most, max=most).astype(kind)


def setup_inputs(seed: int = 0) -> dict:
    streams_of = jax.random.split(jax.random.key(seed), 8)
    hidden_in = draw_hidden_in(jax.random.fold_in(streams_of[7], 71), 0)
    pre_gain = jnp.clip(1.0 + 0.15 * jax.random.normal(streams_of[1], (D,), jnp.float32), 0.25, 1.75)
    w_query = draw_w_query(jax.random.fold_in(streams_of[7], 71), 0)
    w_key = draw_w_key(jax.random.fold_in(streams_of[7], 71), 0)
    w_value = gaussian(streams_of[4], (D, KVHEADS * HEAD), D ** -0.5, 0.09375, ((1, 4),))
    w_out = draw_w_out(jax.random.fold_in(streams_of[7], 71), 0)
    post_gain = jnp.clip(1.0 + 0.15 * jax.random.normal(streams_of[6], (D,), jnp.float32), 0.25, 1.75)
    return {"hidden_in": hidden_in, "pre_gain": pre_gain, "w_query": w_query, "w_key": w_key, "w_value": w_value, "w_out": w_out, "post_gain": post_gain}


def rope_tables(positions):
    index = jnp.arange(0, HEAD, 2).astype(jnp.float32)
    inverse = jnp.exp(-jnp.log(jnp.float32(10000.0)) * index / HEAD)
    angles = positions.astype(jnp.float32)[:, None] * inverse[None, :]
    angles = jnp.concatenate([angles, angles], axis=1)
    return (jnp.cos(angles)[:, None, :], jnp.sin(angles)[:, None, :])

def rotate(values, cosine_table, sine_table):
    half = values.shape[-1] // 2
    turned = jnp.concatenate([-values[..., half:], values[..., :half]], axis=-1)
    return values * cosine_table + turned * sine_table

def reference(hidden_in, pre_gain, w_query, w_key, w_value, w_out, post_gain):
    inputs = hidden_in.astype(jnp.float32)
    normed = (inputs * lax.rsqrt(lax.optimization_barrier(jnp.mean(inputs * inputs, axis=-1, keepdims=True)) + 1e-06) * pre_gain).astype(jnp.bfloat16)
    cosine_table, sine_table = rope_tables(jnp.arange(TOKENS))
    query = jnp.dot(normed, w_query, preferred_element_type=jnp.float32).reshape(TOKENS, QHEADS, HEAD)
    query = rotate(query, cosine_table, sine_table).astype(jnp.bfloat16)
    keys = jnp.dot(normed, w_key, preferred_element_type=jnp.float32).reshape(TOKENS, KVHEADS, HEAD)
    keys = rotate(keys, cosine_table, sine_table).astype(jnp.bfloat16)
    values = jnp.dot(normed, w_value, preferred_element_type=jnp.float32).reshape(TOKENS, KVHEADS, HEAD).astype(jnp.bfloat16)
    padding = jnp.zeros((WINDOW, KVHEADS, HEAD), jnp.bfloat16)
    keys_padded = jnp.concatenate([padding, keys], axis=0)
    values_padded = jnp.concatenate([padding, values], axis=0)
    sink_keys = keys[:SINKS].astype(jnp.float32)
    sink_values = values[:SINKS].astype(jnp.float32)
    group = QHEADS // KVHEADS
    block_rows = min(512, TOKENS)
    span = WINDOW + block_rows

    def one_block(block_index):
        start = (block_index * block_rows).astype(jnp.int32)
        query_block = lax.dynamic_slice_in_dim(query, start, block_rows, 0).astype(jnp.float32).reshape(block_rows, KVHEADS, group, HEAD)
        key_block = lax.dynamic_slice_in_dim(keys_padded, start, span, 0).astype(jnp.float32)
        value_block = lax.dynamic_slice_in_dim(values_padded, start, span, 0).astype(jnp.float32)
        scores = jnp.einsum('qkgd,lkd->kgql', query_block, key_block) / 12.0
        scores = 50.0 * jnp.tanh(scores / 50.0)
        sink_scores = jnp.einsum('qkgd,lkd->kgql', query_block, sink_keys) / 12.0
        sink_scores = 50.0 * jnp.tanh(sink_scores / 50.0)
        query_pos = start + jnp.arange(block_rows, dtype=jnp.int32)
        key_pos = start - WINDOW + jnp.arange(span, dtype=jnp.int32)
        distance = query_pos[:, None] - key_pos[None, :]
        live = (key_pos[None, :] >= SINKS) & (distance >= 0) & (distance < WINDOW)
        sink_live = query_pos[:, None] - jnp.arange(SINKS, dtype=jnp.int32)[None, :] >= 0
        expo = jnp.where(live, jnp.exp(scores), 0.0)
        sink_expo = jnp.where(sink_live, jnp.exp(sink_scores), 0.0)
        total = lax.optimization_barrier(jnp.sum(expo, axis=-1)) + lax.optimization_barrier(jnp.sum(sink_expo, axis=-1))
        weight = expo / total[..., None]
        sink_weight = sink_expo / total[..., None]
        sink_sum = lax.optimization_barrier(jnp.sum(sink_expo, axis=-1))
        weight16 = weight.astype(jnp.bfloat16).astype(jnp.float32)
        sink16 = sink_weight.astype(jnp.bfloat16).astype(jnp.float32)
        attended = jnp.einsum('kgql,lkd->qkgd', weight16, value_block) + jnp.einsum('kgql,lkd->qkgd', sink16, sink_values)
        attended = attended.astype(jnp.bfloat16).reshape(block_rows, QHEADS * HEAD)
        return (attended, lax.optimization_barrier(jnp.sum(sink_sum, axis=(0, 1))))
    attended, sink_sums = lax.map(one_block, jnp.arange(TOKENS // block_rows, dtype=jnp.int32))
    attended = attended.reshape(TOKENS, QHEADS * HEAD)
    sink_sums = sink_sums.reshape(TOKENS)
    projected = jnp.dot(attended, w_out, preferred_element_type=jnp.float32)
    post = projected * lax.rsqrt(lax.optimization_barrier(jnp.mean(projected * projected, axis=-1, keepdims=True)) + 1e-06) * post_gain
    layer_out = (inputs + post).astype(jnp.bfloat16)
    sink_share = jnp.log(sink_sums / QHEADS)
    return (layer_out, sink_share)
```

```python
import functools

import jax
import jax.numpy as jnp
from jax import lax
from jax.experimental import pallas as pl
from jax.experimental.pallas import tpu as pltpu
from jax.sharding import PartitionSpec as P

D = 4608
QHEADS = 16
HEAD = 128
WINDOW = 4096
SINKS = 4


def shifted(x, axis, by):
    devices = lax.axis_size(axis)
    pairs = [(i, i + by) for i in range(devices) if 0 <= i + by < devices]
    return lax.ppermute(x, axis, pairs)


def spread(value, axis, source):
    kept = jnp.where(lax.axis_index(axis) == source, value, 0).astype(value.dtype)
    return lax.psum(kept, axis)


def rope_tables(positions):
    index = jnp.arange(0, HEAD, 2).astype(jnp.float32)
    inverse = jnp.exp(-jnp.log(jnp.float32(10000.0)) * index / HEAD)
    angles = positions.astype(jnp.float32)[:, None] * inverse[None, :]
    angles = jnp.concatenate([angles, angles], axis=1)
    return (jnp.cos(angles)[:, None, :], jnp.sin(angles)[:, None, :])


def rotate(values, cosine_table, sine_table):
    half = values.shape[-1] // 2
    turned = jnp.concatenate([-values[..., half:], values[..., :half]], axis=-1)
    return values * cosine_table + turned * sine_table


def project_keys(states, w_key, w_value, positions):
    count = states.shape[0]
    cosine_table, sine_table = rope_tables(positions)
    keys = jnp.dot(states, w_key, preferred_element_type=jnp.float32).reshape(count, -1, HEAD)
    keys = rotate(keys, cosine_table, sine_table).astype(jnp.bfloat16).reshape(count, -1)
    values = jnp.dot(states, w_value, preferred_element_type=jnp.float32).astype(jnp.bfloat16)
    return (keys, values)


def on_device(hidden_in, pre_gain, w_query, w_key, w_value, w_out, post_gain):
    tok_rows = hidden_in.shape[0]
    local_q = w_query.shape[1] // HEAD
    local_kv = w_key.shape[1] // HEAD
    group = local_q // local_kv
    offset = lax.axis_index("ctx") * tok_rows
    inputs = hidden_in.astype(jnp.float32)
    normed = (
        inputs * lax.rsqrt(jnp.mean(inputs * inputs, axis=-1, keepdims=True) + 1e-06) * pre_gain
    ).astype(jnp.bfloat16)
    positions = offset + jnp.arange(tok_rows, dtype=jnp.int32)
    cosine_table, sine_table = rope_tables(positions)
    query = jnp.dot(normed, w_query, preferred_element_type=jnp.float32).reshape(
        tok_rows, local_q, HEAD
    )
    query = (
        rotate(query, cosine_table, sine_table)
        .astype(jnp.bfloat16)
        .reshape(tok_rows, local_kv, group, HEAD)
    )
    keys, values = project_keys(normed, w_key, w_value, positions)
    reach = WINDOW // tok_rows
    pieces = []
    for distance in range(reach, 0, -1):
        pieces.append(shifted((keys, values), "ctx", distance))
    keys_all = jnp.concatenate([piece[0] for piece in pieces] + [keys], axis=0)
    values_all = jnp.concatenate([piece[1] for piece in pieces] + [values], axis=0)
    sink_keys, sink_values = (spread(keys[:SINKS], "ctx", 0), spread(values[:SINKS], "ctx", 0))
    sink_keys = sink_keys.reshape(SINKS, local_kv, HEAD)
    sink_values = sink_values.reshape(SINKS, local_kv, HEAD)
    block_rows = min(512, tok_rows)
    span = WINDOW + block_rows

    def one_block(block_index):
        start = block_index * block_rows
        key_block = keys_all.reshape(span, local_kv, HEAD)
        value_block = values_all.reshape(span, local_kv, HEAD)
        scores = (
            jnp.einsum("qkgd,lkd->kgql", query, key_block, preferred_element_type=jnp.float32)
            / 12.0
        )
        scores = 50.0 * jnp.tanh(scores / 50.0)
        sink_scores = (
            jnp.einsum("qkgd,lkd->kgql", query, sink_keys, preferred_element_type=jnp.float32)
            / 12.0
        )
        sink_scores = 50.0 * jnp.tanh(sink_scores / 50.0)
        query_pos = offset + start + jnp.arange(block_rows, dtype=jnp.int32)
        key_pos = offset + start - WINDOW + jnp.arange(span, dtype=jnp.int32)
        distance_map = query_pos[:, None] - key_pos[None, :]
        live = (key_pos[None, :] >= SINKS) & (distance_map >= 0) & (distance_map < WINDOW)
        sink_live = query_pos[:, None] - jnp.arange(SINKS, dtype=jnp.int32)[None, :] >= 0
        expo = jnp.where(live, jnp.exp(scores), 0.0)
        sink_expo = jnp.where(sink_live, jnp.exp(sink_scores), 0.0)
        total = jnp.sum(expo, axis=-1) + jnp.sum(sink_expo, axis=-1)
        weight = expo / total[..., None]
        sink_weight = sink_expo / total[..., None]
        sink_sum = jnp.sum(sink_expo, axis=-1)
        attended = jnp.einsum(
            "kgql,lkd->qkgd",
            weight.astype(jnp.bfloat16),
            value_block,
            preferred_element_type=jnp.float32,
        )
        attended = attended + jnp.einsum(
            "kgql,lkd->qkgd",
            sink_weight.astype(jnp.bfloat16),
            sink_values,
            preferred_element_type=jnp.float32,
        )
        attended = attended.astype(jnp.bfloat16).reshape(block_rows, local_q * HEAD)
        return (attended, jnp.sum(sink_sum, axis=(0, 1)))

    attended, sink_sums = lax.map(one_block, jnp.arange(tok_rows // block_rows, dtype=jnp.int32))
    attended = attended.reshape(tok_rows, local_q * HEAD)
    sink_sums = sink_sums.reshape(tok_rows)
    cols_dev = post_gain.shape[0]
    partial_rows = jnp.dot(attended, w_out, preferred_element_type=jnp.float32)
    projected = lax.psum_scatter(partial_rows, "tp", scatter_dimension=1, tiled=True)
    squares = jnp.sum(projected * projected, axis=-1)
    total_squares, total_sinks = lax.psum((squares, sink_sums), "tp")
    post = projected * lax.rsqrt(total_squares / D + 1e-06)[:, None] * post_gain
    own_cols = lax.dynamic_slice_in_dim(inputs, lax.axis_index("tp") * cols_dev, cols_dev, 1)
    layer_out = (own_cols + post).astype(jnp.bfloat16)
    sink_share = jnp.log(total_sinks / QHEADS)
    return (layer_out, sink_share)


MESH = pl.DeviceIdType.MESH
LOG2E = 1.4426950408889634


def expo_of(query, keys):
    scores = lax.dot_general(
        query, keys, (((1,), (1,)), ((), ())), preferred_element_type=jnp.float32
    )
    return jnp.exp2((50.0 * LOG2E) * jnp.tanh(scores * (1.0 / 600.0)))


def fused_kernel(
    n,
    hid_hbm,
    wq_hbm,
    wk_hbm,
    wv_hbm,
    wo_hbm,
    gain_ref,
    post_ref,
    cos_ref,
    sin_ref,
    out_ref,
    share_ref,
    hid,
    normed,
    wq,
    wk,
    wv,
    wo,
    query,
    kv,
    acc,
    sink_acc,
    att,
    proj,
    stat,
    hid_sem,
    w_sem,
    wo_own_sem,
    wo_send,
    wo_recv,
    kv_send_z,
    kv_send_y,
    kv_recv,
    att_send,
    att_recv,
    stat_send,
    stat_recv,
):
    rows, width = hid.shape
    cols = proj.shape[1]
    q_width = query.shape[1]
    kv_width = kv.shape[2] // 2
    heads = q_width // HEAD
    group = q_width // kv_width
    levels = n // 2
    c, t = lax.axis_index("ctx"), lax.axis_index("tp")
    z, y = c // 2, lax.rem(c, 2)
    mate = 2 * z + 1 - y
    t_core = 2 * (t // 2) + 1 - lax.rem(t, 2)
    t_far = lax.rem(t + 2, 4)
    t_diag = lax.rem(t_core + 2, 4)
    chunks = hid_sem.shape[0]
    step_rows = rows // chunks

    def hid_copy(i):
        part = pl.ds(i * step_rows, step_rows)
        return pltpu.make_async_copy(hid_hbm.at[part], hid.at[part], hid_sem.at[i])

    for i in range(chunks):
        hid_copy(i).start()
    weights = [
        pltpu.make_async_copy(a, b, w_sem.at[i])
        for i, (a, b) in enumerate(((wk_hbm, wk), (wv_hbm, wv), (wq_hbm, wq)))
    ]
    for copy in weights:
        copy.start()

    barrier = pltpu.get_barrier_semaphore()
    for other in (t_core, t_far, t_diag):
        pl.semaphore_signal(barrier, inc=1, device_id=(c, other), device_id_type=MESH)
    pl.semaphore_signal(barrier, inc=1, device_id=(mate, t), device_id_type=MESH)

    @pl.when(z > 0)
    def _():
        pl.semaphore_signal(barrier, inc=1, device_id=(c - 2, t), device_id_type=MESH)

    @pl.when(z < levels - 1)
    def _():
        pl.semaphore_signal(barrier, inc=1, device_id=(c + 2, t), device_id_type=MESH)

    pl.semaphore_wait(barrier, 4 + jnp.minimum(z, 1) + jnp.minimum(levels - 1 - z, 1))

    def wo_copy(i, other):
        part = pl.ds(pl.multiple_of(other * cols, 128), cols)
        return pltpu.make_async_remote_copy(
            src_ref=wo_hbm.at[:, part],
            dst_ref=wo.at[t],
            send_sem=wo_send.at[i],
            recv_sem=wo_recv.at[i],
            device_id=(c, other),
            device_id_type=MESH,
        )

    partners = (t_core, t_far, t_diag)
    wo_copies = [wo_copy(i, other) for i, other in enumerate(partners)]
    for i in (1, 2, 0):
        wo_copies[i].start()
    own_wo = pltpu.make_async_copy(
        wo_hbm.at[:, pl.ds(pl.multiple_of(t * cols, 128), cols)], wo.at[t], wo_own_sem
    )
    own_wo.start()

    norm_rows = 32
    for i in range(chunks):
        hid_copy(i).wait()

        def norm_step(r, carry, i=i):
            part = pl.ds(pl.multiple_of(i * step_rows + r * norm_rows, norm_rows), norm_rows)
            x = hid[part, :].astype(jnp.float32)
            scale = lax.rsqrt(jnp.sum(x * x, axis=-1, keepdims=True) * (1.0 / width) + 1e-06)
            normed[part, :] = (x * scale * gain_ref[...]).astype(jnp.bfloat16)
            return carry

        lax.fori_loop(0, step_rows // norm_rows, norm_step, 0)

    def rope(x):
        return x * cos_ref[...] + pltpu.roll(x, HEAD // 2, 1) * sin_ref[...]

    weights[0].wait()
    keys = jnp.dot(normed[...], wk[...], preferred_element_type=jnp.float32)
    for h in range(kv_width // HEAD):
        cut = slice(h * HEAD, (h + 1) * HEAD)
        kv[c, :, cut] = rope(keys[:, cut]).astype(jnp.bfloat16)
    weights[1].wait()
    values = jnp.dot(normed[...], wv[...], preferred_element_type=jnp.float32)
    kv[c, :, kv_width:] = values.astype(jnp.bfloat16)

    def up_copy(b):
        return pltpu.make_async_remote_copy(
            src_ref=kv.at[b],
            dst_ref=kv.at[b],
            send_sem=kv_send_z.at[b],
            recv_sem=kv_recv.at[b],
            device_id=(lax.rem(c + 2, n), t),
            device_id_type=MESH,
        )

    def mate_copy(b):
        return pltpu.make_async_remote_copy(
            src_ref=kv.at[b],
            dst_ref=kv.at[b],
            send_sem=kv_send_y.at[b],
            recv_sem=kv_recv.at[b],
            device_id=(mate, t),
            device_id_type=MESH,
        )

    @pl.when(z < levels - 1)
    def _():
        up_copy(c).start()

    @pl.when(y == 0)
    def _():
        mate_copy(c).start()

    weights[2].wait()

    def query_step(i, carry):
        part = pl.ds(pl.multiple_of(i * kv_width, kv_width), kv_width)
        out = jnp.dot(normed[...], wq[:, part], preferred_element_type=jnp.float32)
        for h in range(kv_width // HEAD):
            cut = slice(h * HEAD, (h + 1) * HEAD)
            here = pl.ds(pl.multiple_of(i * kv_width + h * HEAD, HEAD), HEAD)
            query[:, here] = rope(out[:, cut]).astype(jnp.bfloat16)
        return carry

    lax.fori_loop(0, group, query_step, 0)

    ones = jnp.ones((rows, HEAD), jnp.bfloat16)

    def attend(b, own):
        for h in range(heads):
            k0 = (h // group) * HEAD
            v0 = kv_width + k0
            expo = expo_of(query[:, h * HEAD : (h + 1) * HEAD], kv[b, :, k0 : k0 + HEAD])
            if own:
                at = lax.broadcasted_iota(jnp.int32, (rows, rows), 0)
                key_at = lax.broadcasted_iota(jnp.int32, (rows, rows), 1)
                expo = jnp.where(key_at <= at, expo, 0.0)
            more = jnp.concatenate([kv[b, :, v0 : v0 + HEAD], ones], axis=1)
            part = jnp.dot(expo.astype(jnp.bfloat16), more, preferred_element_type=jnp.float32)
            if own:
                acc[h] = part
            else:
                acc[h] += part

    attend(c, True)

    def level_step(s, carry):
        level = z - s

        @pl.when(s > 0)
        def _():
            b = 2 * level + y
            up_copy(b).wait_recv()

            @pl.when(z < levels - 1)
            def _():
                up_copy(b).start()

            mate_copy(b).start()
            attend(b, False)

        @pl.when((s > 0) | (y == 1))
        def _():
            b = 2 * level + 1 - y
            mate_copy(b).wait_recv()
            attend(b, False)

        return carry

    lax.fori_loop(0, z + 1, level_step, 0)

    def att_copy(kind, h):
        slot = t if kind < 2 else t_far
        return pltpu.make_async_remote_copy(
            src_ref=att.at[slot, h],
            dst_ref=att.at[slot, h],
            send_sem=att_send.at[kind, h],
            recv_sem=att_recv.at[kind, h],
            device_id=(c, t_far if kind == 0 else t_core),
            device_id_type=MESH,
        )

    for h in range(heads):
        att[t, h] = (acc[h, :, :HEAD] / acc[h, :, HEAD:]).astype(jnp.bfloat16)
        att_copy(0, h).start()
        att_copy(1, h).start()

    lane = lax.broadcasted_iota(jnp.int32, (rows, HEAD), 1)
    row = lax.broadcasted_iota(jnp.int32, (rows, HEAD), 0) + c * rows
    sink_live = (lane < SINKS) & (lane <= row)
    sinks = jnp.zeros((rows, HEAD), jnp.float32)
    for h in range(heads):
        k0 = (h // group) * HEAD
        sinks += expo_of(query[:, h * HEAD : (h + 1) * HEAD], kv[0, :HEAD, k0 : k0 + HEAD])
    sink_acc[...] = jnp.where(sink_live, sinks, 0.0)

    tile = cols // 3

    def add_slot(slot, first):
        rows_of = jnp.concatenate([att[slot, h] for h in range(heads)], axis=1)
        for i in range(3):
            cut = slice(i * tile, (i + 1) * tile)
            part = jnp.dot(rows_of, wo[slot, :, cut], preferred_element_type=jnp.float32)
            if first:
                proj[:, cut] = part
            else:
                proj[:, cut] += part

    own_wo.wait()
    add_slot(t, True)
    wo_copies[0].wait_recv()
    for h in range(heads):
        att_copy(1, h).wait_recv()
    add_slot(t_core, False)
    for h in range(heads):
        att_copy(0, h).wait_recv()
        att_copy(2, h).start()
    wo_copies[1].wait_recv()
    add_slot(t_far, False)
    wo_copies[2].wait_recv()
    for h in range(heads):
        att_copy(2, h).wait_recv()
    add_slot(t_diag, False)

    squares = jnp.sum(proj[...] * proj[...], axis=-1, keepdims=True)
    sink_sum = jnp.sum(sink_acc[...], axis=-1, keepdims=True)
    both = jnp.where(lane == 0, squares, sink_sum)
    stat[t] = jnp.transpose(both)[:8, :]

    def stat_copy(i, other):
        return pltpu.make_async_remote_copy(
            src_ref=stat.at[t],
            dst_ref=stat.at[t],
            send_sem=stat_send.at[i],
            recv_sem=stat_recv.at[i],
            device_id=(c, other),
            device_id_type=MESH,
        )

    stats = [stat_copy(i, other) for i, other in enumerate(partners)]
    for copy in stats:
        copy.start()
    for copy in stats:
        copy.wait_recv()
    total = stat[0] + stat[1] + stat[2] + stat[3]
    share_ref[...] = jnp.log(total[1:2, :] / (4.0 * heads))
    column = jnp.transpose(jnp.concatenate([total] * 16, axis=0))[:, :1]
    scale = lax.rsqrt(column / width + 1e-06)
    mine = hid[:, pl.ds(pl.multiple_of(t * cols, 128), cols)].astype(jnp.float32)
    out_ref[...] = (mine + proj[...] * scale * post_ref[...]).astype(jnp.bfloat16)

    @pl.when(z < levels - 1)
    def _():
        up_copy(c).wait_send()

    @pl.when(y == 0)
    def _():
        mate_copy(c).wait_send()

    def drain_step(s, carry):
        b = 2 * (z - s) + y

        @pl.when(z < levels - 1)
        def _():
            up_copy(b).wait_send()

        mate_copy(b).wait_send()
        return carry

    lax.fori_loop(1, z + 1, drain_step, 0)
    for copy in wo_copies + stats:
        copy.wait_send()
    for kind in range(3):
        for h in range(heads):
            att_copy(kind, h).wait_send()


def fused_on_device(n, hidden_in, pre_gain, w_query, w_key, w_value, w_out, post_gain):
    rows, width = hidden_in.shape
    cols = post_gain.shape[0]
    q_width, kv_width = w_query.shape[1], w_key.shape[1]
    heads = q_width // HEAD
    positions = lax.axis_index("ctx") * rows + jnp.arange(rows, dtype=jnp.int32)
    cosine, sine = rope_tables(positions)
    cosine, sine = cosine[:, 0, :], sine[:, 0, :]
    sine = jnp.where(jnp.arange(HEAD)[None, :] < HEAD // 2, -sine, sine)
    hbm, vmem = pl.BlockSpec(memory_space=pl.ANY), pl.BlockSpec(memory_space=pltpu.VMEM)
    dma = pltpu.SemaphoreType.DMA
    bf16, f32 = jnp.bfloat16, jnp.float32
    layer_out, share = pl.pallas_call(
        functools.partial(fused_kernel, n),
        out_shape=(
            jax.ShapeDtypeStruct((rows, cols), bf16),
            jax.ShapeDtypeStruct((1, rows), f32),
        ),
        in_specs=[hbm] * 5 + [vmem] * 4,
        out_specs=(vmem, vmem),
        scratch_shapes=[
            pltpu.VMEM((rows, width), bf16),
            pltpu.VMEM((rows, width), bf16),
            pltpu.VMEM((width, q_width), bf16),
            pltpu.VMEM((width, kv_width), bf16),
            pltpu.VMEM((width, kv_width), bf16),
            pltpu.VMEM((4, q_width, cols), bf16),
            pltpu.VMEM((rows, q_width), bf16),
            pltpu.VMEM((n, rows, 2 * kv_width), bf16),
            pltpu.VMEM((heads, rows, 2 * HEAD), f32),
            pltpu.VMEM((rows, HEAD), f32),
            pltpu.VMEM((4, heads, rows, HEAD), bf16),
            pltpu.VMEM((rows, cols), f32),
            pltpu.VMEM((4, 8, rows), f32),
            dma((4,)),
            dma((3,)),
            dma,
            dma((3,)),
            dma((3,)),
            dma((n,)),
            dma((n,)),
            dma((n,)),
            dma((3, heads)),
            dma((3, heads)),
            dma((3,)),
            dma((3,)),
        ],
        compiler_params=pltpu.CompilerParams(
            collective_id=0, has_side_effects=True, vmem_limit_bytes=56 * 1024 * 1024
        ),
        cost_estimate=pl.CostEstimate(
            flops=2 * rows * width * (q_width + 2 * kv_width)
            + 4 * rows * n * rows * q_width
            + 8 * rows * q_width * cols,
            bytes_accessed=2 * width * (rows + 2 * q_width + 2 * kv_width),
            transcendentals=2 * heads * rows * n * rows,
        ),
    )(
        hidden_in,
        w_query,
        w_key,
        w_value,
        w_out,
        pre_gain.reshape(1, width),
        post_gain.reshape(1, cols),
        cosine,
        sine,
    )
    return layer_out, share.reshape(rows)


def solution(mesh):
    n, tp = mesh.shape["ctx"], mesh.shape["tp"]

    def body(*args):
        if n * args[0].shape[0] <= WINDOW and n % 2 == 0 and tp == 4:
            return fused_on_device(n, *args)
        return on_device(*args)

    return jax.shard_map(
        body,
        mesh=mesh,
        in_specs=(
            P("ctx", None),
            P(),
            P(None, "tp"),
            P(None, "tp"),
            P(None, "tp"),
            P("tp", None),
            P("tp"),
        ),
        out_specs=(P("ctx", "tp"), P("ctx")),
        check_vma=False,
    )
```

```python
import functools

import jax
import jax.numpy as jnp
from jax import lax
from jax.experimental import pallas as pl
from jax.experimental.pallas import tpu as pltpu
from jax.sharding import PartitionSpec as P

D = 4608
QHEADS = 16
HEAD = 128
WINDOW = 4096
SINKS = 4


def shifted(x, axis, by):
    devices = lax.axis_size(axis)
    pairs = [(i, i + by) for i in range(devices) if 0 <= i + by < devices]
    return lax.ppermute(x, axis, pairs)


def spread(value, axis, source):
    kept = jnp.where(lax.axis_index(axis) == source, value, 0).astype(value.dtype)
    return lax.psum(kept, axis)


def rope_tables(positions):
    index = jnp.arange(0, HEAD, 2).astype(jnp.float32)
    inverse = jnp.exp(-jnp.log(jnp.float32(10000.0)) * index / HEAD)
    angles = positions.astype(jnp.float32)[:, None] * inverse[None, :]
    angles = jnp.concatenate([angles, angles], axis=1)
    return (jnp.cos(angles)[:, None, :], jnp.sin(angles)[:, None, :])


def rotate(values, cosine_table, sine_table):
    half = values.shape[-1] // 2
    turned = jnp.concatenate([-values[..., half:], values[..., :half]], axis=-1)
    return values * cosine_table + turned * sine_table


def project_keys(states, w_key, w_value, positions):
    count = states.shape[0]
    cosine_table, sine_table = rope_tables(positions)
    keys = jnp.dot(states, w_key, preferred_element_type=jnp.float32).reshape(count, -1, HEAD)
    keys = rotate(keys, cosine_table, sine_table).astype(jnp.bfloat16).reshape(count, -1)
    values = jnp.dot(states, w_value, preferred_element_type=jnp.float32).astype(jnp.bfloat16)
    return (keys, values)


def on_device(hidden_in, pre_gain, w_query, w_key, w_value, w_out, post_gain):
    tok_rows = hidden_in.shape[0]
    local_q = w_query.shape[1] // HEAD
    local_kv = w_key.shape[1] // HEAD
    group = local_q // local_kv
    offset = lax.axis_index("ctx") * tok_rows
    inputs = hidden_in.astype(jnp.float32)
    normed = (
        inputs * lax.rsqrt(jnp.mean(inputs * inputs, axis=-1, keepdims=True) + 1e-06) * pre_gain
    ).astype(jnp.bfloat16)
    positions = offset + jnp.arange(tok_rows, dtype=jnp.int32)
    cosine_table, sine_table = rope_tables(positions)
    query = jnp.dot(normed, w_query, preferred_element_type=jnp.float32).reshape(
        tok_rows, local_q, HEAD
    )
    query = (
        rotate(query, cosine_table, sine_table)
        .astype(jnp.bfloat16)
        .reshape(tok_rows, local_kv, group, HEAD)
    )
    keys, values = project_keys(normed, w_key, w_value, positions)
    reach = WINDOW // tok_rows
    pieces = []
    for distance in range(reach, 0, -1):
        pieces.append(shifted((keys, values), "ctx", distance))
    keys_all = jnp.concatenate([piece[0] for piece in pieces] + [keys], axis=0)
    values_all = jnp.concatenate([piece[1] for piece in pieces] + [values], axis=0)
    sink_keys, sink_values = (spread(keys[:SINKS], "ctx", 0), spread(values[:SINKS], "ctx", 0))
    sink_keys = sink_keys.reshape(SINKS, local_kv, HEAD)
    sink_values = sink_values.reshape(SINKS, local_kv, HEAD)
    block_rows = min(512, tok_rows)
    span = WINDOW + block_rows

    def one_block(block_index):
        start = block_index * block_rows
        key_block = keys_all.reshape(span, local_kv, HEAD)
        value_block = values_all.reshape(span, local_kv, HEAD)
        scores = (
            jnp.einsum("qkgd,lkd->kgql", query, key_block, preferred_element_type=jnp.float32)
            / 12.0
        )
        scores = 50.0 * jnp.tanh(scores / 50.0)
        sink_scores = (
            jnp.einsum("qkgd,lkd->kgql", query, sink_keys, preferred_element_type=jnp.float32)
            / 12.0
        )
        sink_scores = 50.0 * jnp.tanh(sink_scores / 50.0)
        query_pos = offset + start + jnp.arange(block_rows, dtype=jnp.int32)
        key_pos = offset + start - WINDOW + jnp.arange(span, dtype=jnp.int32)
        distance_map = query_pos[:, None] - key_pos[None, :]
        live = (key_pos[None, :] >= SINKS) & (distance_map >= 0) & (distance_map < WINDOW)
        sink_live = query_pos[:, None] - jnp.arange(SINKS, dtype=jnp.int32)[None, :] >= 0
        expo = jnp.where(live, jnp.exp(scores), 0.0)
        sink_expo = jnp.where(sink_live, jnp.exp(sink_scores), 0.0)
        total = jnp.sum(expo, axis=-1) + jnp.sum(sink_expo, axis=-1)
        weight = expo / total[..., None]
        sink_weight = sink_expo / total[..., None]
        sink_sum = jnp.sum(sink_expo, axis=-1)
        attended = jnp.einsum(
            "kgql,lkd->qkgd",
            weight.astype(jnp.bfloat16),
            value_block,
            preferred_element_type=jnp.float32,
        )
        attended = attended + jnp.einsum(
            "kgql,lkd->qkgd",
            sink_weight.astype(jnp.bfloat16),
            sink_values,
            preferred_element_type=jnp.float32,
        )
        attended = attended.astype(jnp.bfloat16).reshape(block_rows, local_q * HEAD)
        return (attended, jnp.sum(sink_sum, axis=(0, 1)))

    attended, sink_sums = lax.map(one_block, jnp.arange(tok_rows // block_rows, dtype=jnp.int32))
    attended = attended.reshape(tok_rows, local_q * HEAD)
    sink_sums = sink_sums.reshape(tok_rows)
    cols_dev = post_gain.shape[0]
    partial_rows = jnp.dot(attended, w_out, preferred_element_type=jnp.float32)
    projected = lax.psum_scatter(partial_rows, "tp", scatter_dimension=1, tiled=True)
    squares = jnp.sum(projected * projected, axis=-1)
    total_squares, total_sinks = lax.psum((squares, sink_sums), "tp")
    post = projected * lax.rsqrt(total_squares / D + 1e-06)[:, None] * post_gain
    own_cols = lax.dynamic_slice_in_dim(inputs, lax.axis_index("tp") * cols_dev, cols_dev, 1)
    layer_out = (own_cols + post).astype(jnp.bfloat16)
    sink_share = jnp.log(total_sinks / QHEADS)
    return (layer_out, sink_share)


MESH = pl.DeviceIdType.MESH
LOG2E = 1.4426950408889634


def expo_of(query, keys):
    scores = lax.dot_general(
        query, keys, (((1,), (1,)), ((), ())), preferred_element_type=jnp.float32
    )
    return jnp.exp2((50.0 * LOG2E) * jnp.tanh(scores * (1.0 / 600.0)))


def fused_kernel(
    n,
    hid_hbm,
    wq_hbm,
    wk_hbm,
    wv_hbm,
    wo_hbm,
    gain_ref,
    post_ref,
    cos_ref,
    sin_ref,
    out_ref,
    share_ref,
    hid,
    normed,
    wq,
    wk,
    wv,
    wo,
    query,
    kv,
    acc,
    sink_acc,
    att,
    proj,
    stat,
    hid_sem,
    w_sem,
    wo_own_sem,
    wo_send,
    wo_recv,
    kv_send_z,
    kv_send_y,
    kv_recv,
    v_send,
    v_recv,
    tail_send,
    tail_recv,
    end_send,
    down_send,
    end_recv,
    att_send,
    att_recv,
    stat_send,
    stat_recv,
):
    rows, width = hid.shape
    cols = proj.shape[1]
    q_width = query.shape[1]
    kv_width = kv.shape[2] // 2
    heads = q_width // HEAD
    group = q_width // kv_width
    levels = n // 2
    c, t = lax.axis_index("ctx"), lax.axis_index("tp")
    z, y = c // 2, lax.rem(c, 2)
    mate = 2 * z + 1 - y
    t_core = 2 * (t // 2) + 1 - lax.rem(t, 2)
    t_far = lax.rem(t + 2, 4)
    t_diag = lax.rem(t_core + 2, 4)
    chunks = hid_sem.shape[0]
    step_rows = rows // chunks

    def hid_copy(i):
        part = pl.ds(i * step_rows, step_rows)
        return pltpu.make_async_copy(hid_hbm.at[part], hid.at[part], hid_sem.at[i])

    for i in range(chunks):
        hid_copy(i).start()
    weights = [
        pltpu.make_async_copy(a, b, w_sem.at[i])
        for i, (a, b) in enumerate(((wk_hbm, wk), (wv_hbm, wv), (wq_hbm, wq)))
    ]
    for copy in weights:
        copy.start()

    barrier = pltpu.get_barrier_semaphore()
    for other in (t_core, t_far, t_diag):
        pl.semaphore_signal(barrier, inc=1, device_id=(c, other), device_id_type=MESH)
    pl.semaphore_signal(barrier, inc=1, device_id=(mate, t), device_id_type=MESH)

    @pl.when(z > 0)
    def _():
        pl.semaphore_signal(barrier, inc=1, device_id=(c - 2, t), device_id_type=MESH)

    @pl.when(z < levels - 1)
    def _():
        pl.semaphore_signal(barrier, inc=1, device_id=(c + 2, t), device_id_type=MESH)

    pl.semaphore_wait(barrier, 4 + jnp.minimum(z, 1) + jnp.minimum(levels - 1 - z, 1))

    end = q_width // 8
    bulk = q_width - 2 * end

    def wo_copy(i, other):
        part = pl.ds(pl.multiple_of(other * cols, 128), cols)
        span = pl.ds(0, q_width if i == 0 else bulk)
        return pltpu.make_async_remote_copy(
            src_ref=wo_hbm.at[span, part],
            dst_ref=wo.at[t, span],
            send_sem=wo_send.at[i],
            recv_sem=wo_recv.at[i],
            device_id=(c, other),
            device_id_type=MESH,
        )

    partners = (t_core, t_far, t_diag)
    wo_copies = [wo_copy(i, other) for i, other in enumerate(partners)]

    def tail_copy(i, other):
        part = pl.ds(pl.multiple_of(other * cols, 128), cols)
        span = pl.ds(pl.multiple_of(bulk + end * (1 - jnp.minimum(z, 1)), 16), end)
        return pltpu.make_async_remote_copy(
            src_ref=wo_hbm.at[span, part],
            dst_ref=wo.at[t, span],
            send_sem=tail_send.at[i],
            recv_sem=tail_recv.at[i],
            device_id=(c, other),
            device_id_type=MESH,
        )

    def end_copy(i, up):
        slot = (t_far, t_diag)[i]
        span = pl.ds(bulk + end if up else bulk, end)
        return pltpu.make_async_remote_copy(
            src_ref=wo.at[slot, span],
            dst_ref=wo.at[slot, span],
            send_sem=end_send.at[i] if up else down_send.at[i],
            recv_sem=end_recv.at[i],
            device_id=(lax.rem(c + 2 if up else c + n - 2, n), t),
            device_id_type=MESH,
        )

    tails = [tail_copy(0, t_far), tail_copy(1, t_diag)]
    for copy in tails:
        copy.start()
    for i in (1, 2, 0):
        wo_copies[i].start()
    own_wo = pltpu.make_async_copy(
        wo_hbm.at[:, pl.ds(pl.multiple_of(t * cols, 128), cols)], wo.at[t], wo_own_sem
    )
    own_wo.start()

    norm_rows = 32
    for i in range(chunks):
        hid_copy(i).wait()

        def norm_step(r, carry, i=i):
            part = pl.ds(pl.multiple_of(i * step_rows + r * norm_rows, norm_rows), norm_rows)
            x = hid[part, :].astype(jnp.float32)
            scale = lax.rsqrt(jnp.sum(x * x, axis=-1, keepdims=True) * (1.0 / width) + 1e-06)
            normed[part, :] = (x * scale * gain_ref[...].reshape(1, width)).astype(jnp.bfloat16)
            return carry

        lax.fori_loop(0, step_rows // norm_rows, norm_step, 0)

    def rope(x):
        return x * cos_ref[...] + pltpu.roll(x, HEAD // 2, 1) * sin_ref[...]

    weights[0].wait()
    keys = jnp.dot(normed[...], wk[...], preferred_element_type=jnp.float32)
    for h in range(kv_width // HEAD):
        cut = slice(h * HEAD, (h + 1) * HEAD)
        kv[c, :, cut] = rope(keys[:, cut]).astype(jnp.bfloat16)
    weights[1].wait()
    values = jnp.dot(normed[...], wv[...], preferred_element_type=jnp.float32)
    kv[c, :, kv_width:] = values.astype(jnp.bfloat16)

    def up_copy(b):
        return pltpu.make_async_remote_copy(
            src_ref=kv.at[b],
            dst_ref=kv.at[b],
            send_sem=kv_send_z.at[b],
            recv_sem=kv_recv.at[b],
            device_id=(lax.rem(c + 2, n), t),
            device_id_type=MESH,
        )

    def mate_copy(b):
        return pltpu.make_async_remote_copy(
            src_ref=kv.at[b],
            dst_ref=kv.at[b],
            send_sem=kv_send_y.at[b],
            recv_sem=kv_recv.at[b],
            device_id=(mate, t),
            device_id_type=MESH,
        )

    def mate_keys(b):
        part = pl.ds(0, kv_width)
        return pltpu.make_async_remote_copy(
            src_ref=kv.at[b, :, part],
            dst_ref=kv.at[b, :, part],
            send_sem=kv_send_y.at[b],
            recv_sem=kv_recv.at[b],
            device_id=(mate, t),
            device_id_type=MESH,
        )

    def up_values(b):
        part = pl.ds(kv_width, kv_width)
        return pltpu.make_async_remote_copy(
            src_ref=kv.at[b, :, part],
            dst_ref=kv.at[b, :, part],
            send_sem=v_send,
            recv_sem=v_recv,
            device_id=(lax.rem(c + 2, n), t),
            device_id_type=MESH,
        )

    @pl.when(z < levels - 1)
    def _():
        up_copy(c).start()

    @pl.when(y == 0)
    def _():
        mate_copy(c).start()

    weights[2].wait()

    def query_step(i, carry):
        part = pl.ds(pl.multiple_of(i * kv_width, kv_width), kv_width)
        out = jnp.dot(normed[...], wq[:, part], preferred_element_type=jnp.float32)
        for h in range(kv_width // HEAD):
            cut = slice(h * HEAD, (h + 1) * HEAD)
            here = pl.ds(pl.multiple_of(i * kv_width + h * HEAD, HEAD), HEAD)
            query[:, here] = rope(out[:, cut]).astype(jnp.bfloat16)
        return carry

    lax.fori_loop(0, group, query_step, 0)

    ones = jnp.ones((rows, HEAD), jnp.bfloat16)

    def attend(b, own):
        for h in range(heads):
            k0 = (h // group) * HEAD
            v0 = kv_width + k0
            expo = expo_of(query[:, h * HEAD : (h + 1) * HEAD], kv[b, :, k0 : k0 + HEAD])
            if own:
                at = lax.broadcasted_iota(jnp.int32, (rows, rows), 0)
                key_at = lax.broadcasted_iota(jnp.int32, (rows, rows), 1)
                expo = jnp.where(key_at <= at, expo, 0.0)
            more = jnp.concatenate([kv[b, :, v0 : v0 + HEAD], ones], axis=1)
            part = jnp.dot(expo.astype(jnp.bfloat16), more, preferred_element_type=jnp.float32)
            if own:
                acc[h] = part
            else:
                acc[h] += part

    attend(c, True)

    def level_step(s, carry):
        level = z - s

        @pl.when(s > 0)
        def _():
            b = 2 * level + y
            up_copy(b).wait_recv()

            @pl.when(z < levels - 1)
            def _():
                up_copy(b).start()

            half = (s == 1) & (y == 0)

            @pl.when(half)
            def _():
                mate_keys(b).start()

            @pl.when(jnp.logical_not(half))
            def _():
                mate_copy(b).start()

            attend(b, False)

        @pl.when((s > 0) | (y == 1))
        def _():
            b = 2 * level + 1 - y
            half = (s == 1) & (y == 1)

            @pl.when(half)
            def _():
                mate_keys(b).wait_recv()
                up_values(b).wait_recv()

            @pl.when(jnp.logical_not(half))
            def _():
                mate_copy(b).wait_recv()

            @pl.when((s == 0) & (z < levels - 1))
            def _():
                up_values(b).start()

            attend(b, False)

        return carry

    lax.fori_loop(0, z + 1, level_step, 0)

    def att_copy(kind, h):
        slot = t if kind < 2 else t_far
        return pltpu.make_async_remote_copy(
            src_ref=att.at[slot, h],
            dst_ref=att.at[slot, h],
            send_sem=att_send.at[kind, h],
            recv_sem=att_recv.at[kind, h],
            device_id=(c, t_far if kind == 0 else t_core),
            device_id_type=MESH,
        )

    for h in range(heads):
        att[t, h] = (acc[h, :, :HEAD] / acc[h, :, HEAD:]).astype(jnp.bfloat16)
        att_copy(0, h).start()
        att_copy(1, h).start()

    for copy in tails:
        copy.wait_recv()

    @pl.when(z == 1)
    def _():
        end_copy(0, False).start()
        end_copy(1, False).start()

    @pl.when(z > 0)
    def _():
        end_copy(0, True).wait_recv()
        end_copy(1, True).wait_recv()

    @pl.when(z < levels - 1)
    def _():
        end_copy(0, True).start()
        end_copy(1, True).start()

    lane = lax.broadcasted_iota(jnp.int32, (rows, HEAD), 1)
    row = lax.broadcasted_iota(jnp.int32, (rows, HEAD), 0) + c * rows
    sink_live = (lane < SINKS) & (lane <= row)
    sinks = jnp.zeros((rows, HEAD), jnp.float32)
    for h in range(heads):
        k0 = (h // group) * HEAD
        sinks += expo_of(query[:, h * HEAD : (h + 1) * HEAD], kv[0, :HEAD, k0 : k0 + HEAD])
    sink_acc[...] = jnp.where(sink_live, sinks, 0.0)

    tile = cols // 3

    def add_slot(slot, first):
        rows_of = jnp.concatenate([att[slot, h] for h in range(heads)], axis=1)
        for i in range(3):
            cut = slice(i * tile, (i + 1) * tile)
            part = jnp.dot(rows_of, wo[slot, :, cut], preferred_element_type=jnp.float32)
            if first:
                proj[:, cut] = part
            else:
                proj[:, cut] += part

    own_wo.wait()
    add_slot(t, True)
    wo_copies[0].wait_recv()
    for h in range(heads):
        att_copy(1, h).wait_recv()
    add_slot(t_core, False)
    for h in range(heads):
        att_copy(0, h).wait_recv()
        att_copy(2, h).start()
    wo_copies[1].wait_recv()

    @pl.when(z == 0)
    def _():
        end_copy(0, False).wait_recv()
        end_copy(1, False).wait_recv()

    add_slot(t_far, False)
    wo_copies[2].wait_recv()
    for h in range(heads):
        att_copy(2, h).wait_recv()
    add_slot(t_diag, False)

    squares = jnp.sum(proj[...] * proj[...], axis=-1, keepdims=True)
    sink_sum = jnp.sum(sink_acc[...], axis=-1, keepdims=True)
    both = jnp.where(lane == 0, squares, sink_sum)
    stat[t] = jnp.transpose(both)[:8, :]

    def stat_copy(i, other):
        return pltpu.make_async_remote_copy(
            src_ref=stat.at[t],
            dst_ref=stat.at[t],
            send_sem=stat_send.at[i],
            recv_sem=stat_recv.at[i],
            device_id=(c, other),
            device_id_type=MESH,
        )

    stats = [stat_copy(i, other) for i, other in enumerate(partners)]
    for copy in stats:
        copy.start()
    for copy in stats:
        copy.wait_recv()
    total = stat[0] + stat[1] + stat[2] + stat[3]
    share_ref[...] = jnp.log(total[1:2, :] / (4.0 * heads))
    column = jnp.transpose(jnp.concatenate([total] * 16, axis=0))[:, :1]
    scale = lax.rsqrt(column / width + 1e-06)
    mine = hid[:, pl.ds(pl.multiple_of(t * cols, 128), cols)].astype(jnp.float32)
    out_ref[...] = (mine + proj[...] * scale * post_ref[...].reshape(1, cols)).astype(jnp.bfloat16)

    @pl.when(z < levels - 1)
    def _():
        up_copy(c).wait_send()
        end_copy(0, True).wait_send()
        end_copy(1, True).wait_send()

    @pl.when((z < levels - 1) & (y == 1))
    def _():
        up_values(c - 1).wait_send()

    @pl.when(z == 1)
    def _():
        end_copy(0, False).wait_send()
        end_copy(1, False).wait_send()

    @pl.when(y == 0)
    def _():
        mate_copy(c).wait_send()

    def drain_step(s, carry):
        b = 2 * (z - s) + y

        @pl.when(z < levels - 1)
        def _():
            up_copy(b).wait_send()

        half = (s == 1) & (y == 0)

        @pl.when(half)
        def _():
            mate_keys(b).wait_send()

        @pl.when(jnp.logical_not(half))
        def _():
            mate_copy(b).wait_send()

        return carry

    lax.fori_loop(1, z + 1, drain_step, 0)
    for copy in wo_copies + tails + stats:
        copy.wait_send()
    for kind in range(3):
        for h in range(heads):
            att_copy(kind, h).wait_send()


def fused_on_device(n, hidden_in, pre_gain, w_query, w_key, w_value, w_out, post_gain):
    rows, width = hidden_in.shape
    cols = post_gain.shape[0]
    q_width, kv_width = w_query.shape[1], w_key.shape[1]
    heads = q_width // HEAD
    positions = lax.axis_index("ctx") * rows + jnp.arange(rows, dtype=jnp.int32)
    cosine, sine = rope_tables(positions)
    cosine, sine = cosine[:, 0, :], sine[:, 0, :]
    sine = jnp.where(jnp.arange(HEAD)[None, :] < HEAD // 2, -sine, sine)
    hbm, vmem = pl.BlockSpec(memory_space=pl.ANY), pl.BlockSpec(memory_space=pltpu.VMEM)
    dma = pltpu.SemaphoreType.DMA
    bf16, f32 = jnp.bfloat16, jnp.float32
    layer_out, share = pl.pallas_call(
        functools.partial(fused_kernel, n),
        out_shape=(
            jax.ShapeDtypeStruct((rows, cols), bf16),
            jax.ShapeDtypeStruct((1, rows), f32),
        ),
        in_specs=[hbm] * 5 + [vmem] * 4,
        out_specs=(vmem, vmem),
        scratch_shapes=[
            pltpu.VMEM((rows, width), bf16),
            pltpu.VMEM((rows, width), bf16),
            pltpu.VMEM((width, q_width), bf16),
            pltpu.VMEM((width, kv_width), bf16),
            pltpu.VMEM((width, kv_width), bf16),
            pltpu.VMEM((4, q_width, cols), bf16),
            pltpu.VMEM((rows, q_width), bf16),
            pltpu.VMEM((n, rows, 2 * kv_width), bf16),
            pltpu.VMEM((heads, rows, 2 * HEAD), f32),
            pltpu.VMEM((rows, HEAD), f32),
            pltpu.VMEM((4, heads, rows, HEAD), bf16),
            pltpu.VMEM((rows, cols), f32),
            pltpu.VMEM((4, 8, rows), f32),
            dma((4,)),
            dma((3,)),
            dma,
            dma((3,)),
            dma((3,)),
            dma((n,)),
            dma((n,)),
            dma((n,)),
            dma,
            dma,
            dma((2,)),
            dma((2,)),
            dma((2,)),
            dma((2,)),
            dma((2,)),
            dma((3, heads)),
            dma((3, heads)),
            dma((3,)),
            dma((3,)),
        ],
        compiler_params=pltpu.CompilerParams(
            collective_id=0, has_side_effects=True, vmem_limit_bytes=56 * 1024 * 1024
        ),
        cost_estimate=pl.CostEstimate(
            flops=2 * rows * width * (q_width + 2 * kv_width)
            + 4 * rows * n * rows * q_width
            + 8 * rows * q_width * cols,
            bytes_accessed=2 * width * (rows + 2 * q_width + 2 * kv_width),
            transcendentals=2 * heads * rows * n * rows,
        ),
    )(
        hidden_in,
        w_query,
        w_key,
        w_value,
        w_out,
        pre_gain,
        post_gain,
        cosine,
        sine,
    )
    return layer_out, share.reshape(rows)


def solution(mesh):
    n, tp = mesh.shape["ctx"], mesh.shape["tp"]

    def body(*args):
        if n * args[0].shape[0] <= WINDOW and n % 2 == 0 and n >= 4 and tp == 4:
            return fused_on_device(n, *args)
        return on_device(*args)

    return jax.shard_map(
        body,
        mesh=mesh,
        in_specs=(
            P("ctx", None),
            P(),
            P(None, "tp"),
            P(None, "tp"),
            P(None, "tp"),
            P("tp", None),
            P("tp"),
        ),
        out_specs=(P("ctx", "tp"), P("ctx")),
        check_vma=False,
    )
```

```python
import functools

import jax
import jax.numpy as jnp
from jax import lax
from jax.experimental import pallas as pl
from jax.experimental.pallas import tpu as pltpu
from jax.sharding import PartitionSpec as P

D = 4608
QHEADS = 16
HEAD = 128
WINDOW = 4096
SINKS = 4


def shifted(x, axis, by):
    devices = lax.axis_size(axis)
    pairs = [(i, i + by) for i in range(devices) if 0 <= i + by < devices]
    return lax.ppermute(x, axis, pairs)


def spread(value, axis, source):
    kept = jnp.where(lax.axis_index(axis) == source, value, 0).astype(value.dtype)
    return lax.psum(kept, axis)


def rope_tables(positions):
    index = jnp.arange(0, HEAD, 2).astype(jnp.float32)
    inverse = jnp.exp(-jnp.log(jnp.float32(10000.0)) * index / HEAD)
    angles = positions.astype(jnp.float32)[:, None] * inverse[None, :]
    angles = jnp.concatenate([angles, angles], axis=1)
    return (jnp.cos(angles)[:, None, :], jnp.sin(angles)[:, None, :])


def rotate(values, cosine_table, sine_table):
    half = values.shape[-1] // 2
    turned = jnp.concatenate([-values[..., half:], values[..., :half]], axis=-1)
    return values * cosine_table + turned * sine_table


def project_keys(states, w_key, w_value, positions):
    count = states.shape[0]
    cosine_table, sine_table = rope_tables(positions)
    keys = jnp.dot(states, w_key, preferred_element_type=jnp.float32).reshape(count, -1, HEAD)
    keys = rotate(keys, cosine_table, sine_table).astype(jnp.bfloat16).reshape(count, -1)
    values = jnp.dot(states, w_value, preferred_element_type=jnp.float32).astype(jnp.bfloat16)
    return (keys, values)


def on_device(hidden_in, pre_gain, w_query, w_key, w_value, w_out, post_gain):
    tok_rows = hidden_in.shape[0]
    local_q = w_query.shape[1] // HEAD
    local_kv = w_key.shape[1] // HEAD
    group = local_q // local_kv
    offset = lax.axis_index("ctx") * tok_rows
    inputs = hidden_in.astype(jnp.float32)
    normed = (
        inputs * lax.rsqrt(jnp.mean(inputs * inputs, axis=-1, keepdims=True) + 1e-06) * pre_gain
    ).astype(jnp.bfloat16)
    positions = offset + jnp.arange(tok_rows, dtype=jnp.int32)
    cosine_table, sine_table = rope_tables(positions)
    query = jnp.dot(normed, w_query, preferred_element_type=jnp.float32).reshape(
        tok_rows, local_q, HEAD
    )
    query = (
        rotate(query, cosine_table, sine_table)
        .astype(jnp.bfloat16)
        .reshape(tok_rows, local_kv, group, HEAD)
    )
    keys, values = project_keys(normed, w_key, w_value, positions)
    reach = WINDOW // tok_rows
    pieces = []
    for distance in range(reach, 0, -1):
        pieces.append(shifted((keys, values), "ctx", distance))
    keys_all = jnp.concatenate([piece[0] for piece in pieces] + [keys], axis=0)
    values_all = jnp.concatenate([piece[1] for piece in pieces] + [values], axis=0)
    sink_keys, sink_values = (spread(keys[:SINKS], "ctx", 0), spread(values[:SINKS], "ctx", 0))
    sink_keys = sink_keys.reshape(SINKS, local_kv, HEAD)
    sink_values = sink_values.reshape(SINKS, local_kv, HEAD)
    block_rows = min(512, tok_rows)
    span = WINDOW + block_rows

    def one_block(block_index):
        start = block_index * block_rows
        key_block = keys_all.reshape(span, local_kv, HEAD)
        value_block = values_all.reshape(span, local_kv, HEAD)
        scores = (
            jnp.einsum("qkgd,lkd->kgql", query, key_block, preferred_element_type=jnp.float32)
            / 12.0
        )
        scores = 50.0 * jnp.tanh(scores / 50.0)
        sink_scores = (
            jnp.einsum("qkgd,lkd->kgql", query, sink_keys, preferred_element_type=jnp.float32)
            / 12.0
        )
        sink_scores = 50.0 * jnp.tanh(sink_scores / 50.0)
        query_pos = offset + start + jnp.arange(block_rows, dtype=jnp.int32)
        key_pos = offset + start - WINDOW + jnp.arange(span, dtype=jnp.int32)
        distance_map = query_pos[:, None] - key_pos[None, :]
        live = (key_pos[None, :] >= SINKS) & (distance_map >= 0) & (distance_map < WINDOW)
        sink_live = query_pos[:, None] - jnp.arange(SINKS, dtype=jnp.int32)[None, :] >= 0
        expo = jnp.where(live, jnp.exp(scores), 0.0)
        sink_expo = jnp.where(sink_live, jnp.exp(sink_scores), 0.0)
        total = jnp.sum(expo, axis=-1) + jnp.sum(sink_expo, axis=-1)
        weight = expo / total[..., None]
        sink_weight = sink_expo / total[..., None]
        sink_sum = jnp.sum(sink_expo, axis=-1)
        attended = jnp.einsum(
            "kgql,lkd->qkgd",
            weight.astype(jnp.bfloat16),
            value_block,
            preferred_element_type=jnp.float32,
        )
        attended = attended + jnp.einsum(
            "kgql,lkd->qkgd",
            sink_weight.astype(jnp.bfloat16),
            sink_values,
            preferred_element_type=jnp.float32,
        )
        attended = attended.astype(jnp.bfloat16).reshape(block_rows, local_q * HEAD)
        return (attended, jnp.sum(sink_sum, axis=(0, 1)))

    attended, sink_sums = lax.map(one_block, jnp.arange(tok_rows // block_rows, dtype=jnp.int32))
    attended = attended.reshape(tok_rows, local_q * HEAD)
    sink_sums = sink_sums.reshape(tok_rows)
    cols_dev = post_gain.shape[0]
    partial_rows = jnp.dot(attended, w_out, preferred_element_type=jnp.float32)
    projected = lax.psum_scatter(partial_rows, "tp", scatter_dimension=1, tiled=True)
    squares = jnp.sum(projected * projected, axis=-1)
    total_squares, total_sinks = lax.psum((squares, sink_sums), "tp")
    post = projected * lax.rsqrt(total_squares / D + 1e-06)[:, None] * post_gain
    own_cols = lax.dynamic_slice_in_dim(inputs, lax.axis_index("tp") * cols_dev, cols_dev, 1)
    layer_out = (own_cols + post).astype(jnp.bfloat16)
    sink_share = jnp.log(total_sinks / QHEADS)
    return (layer_out, sink_share)


MESH = pl.DeviceIdType.MESH
LOG2E = 1.4426950408889634


def expo_of(query, keys):
    scores = lax.dot_general(
        query, keys, (((1,), (1,)), ((), ())), preferred_element_type=jnp.float32
    )
    return jnp.exp2((50.0 * LOG2E) * jnp.tanh(scores * (1.0 / 600.0)))


def fused_kernel(
    n,
    hid_hbm,
    wq_hbm,
    wk_hbm,
    wv_hbm,
    wo_hbm,
    gain_ref,
    post_ref,
    cos_ref,
    sin_ref,
    out_ref,
    share_ref,
    hid,
    normed,
    wq,
    wk,
    wv,
    wo,
    query,
    kv,
    acc,
    sink_acc,
    att,
    proj,
    stat,
    hid_sem,
    w_sem,
    wo_own_sem,
    wo_send,
    wo_recv,
    kv_send_z,
    kv_send_y,
    kv_recv,
    tail_send,
    tail_recv,
    end_send,
    down_send,
    end_recv,
    att_send,
    att_recv,
    stat_send,
    stat_recv,
):
    rows, width = hid.shape
    cols = proj.shape[1]
    q_width = query.shape[1]
    kv_width = kv.shape[2] // 2
    heads = q_width // HEAD
    group = q_width // kv_width
    levels = n // 2
    c, t = lax.axis_index("ctx"), lax.axis_index("tp")
    z, y = c // 2, lax.rem(c, 2)
    mate = 2 * z + 1 - y
    t_core = 2 * (t // 2) + 1 - lax.rem(t, 2)
    t_far = lax.rem(t + 2, 4)
    t_diag = lax.rem(t_core + 2, 4)
    chunks = hid_sem.shape[0]
    step_rows = rows // chunks

    def hid_copy(i):
        part = pl.ds(i * step_rows, step_rows)
        return pltpu.make_async_copy(hid_hbm.at[part], hid.at[part], hid_sem.at[i])

    for i in range(chunks):
        hid_copy(i).start()
    weights = [
        pltpu.make_async_copy(a, b, w_sem.at[i])
        for i, (a, b) in enumerate(((wk_hbm, wk), (wv_hbm, wv), (wq_hbm, wq)))
    ]
    for copy in weights:
        copy.start()

    barrier = pltpu.get_barrier_semaphore()
    for other in (t_core, t_far, t_diag):
        pl.semaphore_signal(barrier, inc=1, device_id=(c, other), device_id_type=MESH)
    pl.semaphore_signal(barrier, inc=1, device_id=(mate, t), device_id_type=MESH)

    @pl.when(z > 0)
    def _():
        pl.semaphore_signal(barrier, inc=1, device_id=(c - 2, t), device_id_type=MESH)

    @pl.when(z < levels - 1)
    def _():
        pl.semaphore_signal(barrier, inc=1, device_id=(c + 2, t), device_id_type=MESH)

    pl.semaphore_wait(barrier, 4 + jnp.minimum(z, 1) + jnp.minimum(levels - 1 - z, 1))

    end = q_width // 8
    bulk = q_width - 2 * end

    def wo_copy(i, other):
        part = pl.ds(pl.multiple_of(other * cols, 128), cols)
        span = pl.ds(0, q_width if i == 0 else bulk)
        return pltpu.make_async_remote_copy(
            src_ref=wo_hbm.at[span, part],
            dst_ref=wo.at[t, span],
            send_sem=wo_send.at[i],
            recv_sem=wo_recv.at[i],
            device_id=(c, other),
            device_id_type=MESH,
        )

    partners = (t_core, t_far, t_diag)
    wo_copies = [wo_copy(i, other) for i, other in enumerate(partners)]

    def tail_copy(i, other):
        part = pl.ds(pl.multiple_of(other * cols, 128), cols)
        span = pl.ds(pl.multiple_of(bulk + end * (1 - jnp.minimum(z, 1)), 16), end)
        return pltpu.make_async_remote_copy(
            src_ref=wo_hbm.at[span, part],
            dst_ref=wo.at[t, span],
            send_sem=tail_send.at[i],
            recv_sem=tail_recv.at[i],
            device_id=(c, other),
            device_id_type=MESH,
        )

    def end_copy(i, up):
        slot = (t_far, t_diag)[i]
        span = pl.ds(bulk + end if up else bulk, end)
        return pltpu.make_async_remote_copy(
            src_ref=wo.at[slot, span],
            dst_ref=wo.at[slot, span],
            send_sem=end_send.at[i] if up else down_send.at[i],
            recv_sem=end_recv.at[i],
            device_id=(lax.rem(c + 2 if up else c + n - 2, n), t),
            device_id_type=MESH,
        )

    tails = [tail_copy(0, t_far), tail_copy(1, t_diag)]
    for copy in tails:
        copy.start()
    for i in (1, 2, 0):
        wo_copies[i].start()
    own_wo = pltpu.make_async_copy(
        wo_hbm.at[:, pl.ds(pl.multiple_of(t * cols, 128), cols)], wo.at[t], wo_own_sem
    )
    own_wo.start()

    norm_rows = 32
    for i in range(chunks):
        hid_copy(i).wait()

        def norm_step(r, carry, i=i):
            part = pl.ds(pl.multiple_of(i * step_rows + r * norm_rows, norm_rows), norm_rows)
            x = hid[part, :].astype(jnp.float32)
            scale = lax.rsqrt(jnp.sum(x * x, axis=-1, keepdims=True) * (1.0 / width) + 1e-06)
            normed[part, :] = (x * scale * gain_ref[...].reshape(1, width)).astype(jnp.bfloat16)
            return carry

        lax.fori_loop(0, step_rows // norm_rows, norm_step, 0)

    def rope(x):
        return x * cos_ref[...] + pltpu.roll(x, HEAD // 2, 1) * sin_ref[...]

    weights[0].wait()
    keys = jnp.dot(normed[...], wk[...], preferred_element_type=jnp.float32)
    for h in range(kv_width // HEAD):
        cut = slice(h * HEAD, (h + 1) * HEAD)
        kv[c, :, cut] = rope(keys[:, cut]).astype(jnp.bfloat16)
    weights[1].wait()
    values = jnp.dot(normed[...], wv[...], preferred_element_type=jnp.float32)
    kv[c, :, kv_width:] = values.astype(jnp.bfloat16)

    def up_copy(b):
        return pltpu.make_async_remote_copy(
            src_ref=kv.at[b],
            dst_ref=kv.at[b],
            send_sem=kv_send_z.at[b],
            recv_sem=kv_recv.at[b],
            device_id=(lax.rem(c + 2, n), t),
            device_id_type=MESH,
        )

    def mate_copy(b):
        return pltpu.make_async_remote_copy(
            src_ref=kv.at[b],
            dst_ref=kv.at[b],
            send_sem=kv_send_y.at[b],
            recv_sem=kv_recv.at[b],
            device_id=(mate, t),
            device_id_type=MESH,
        )

    @pl.when(z < levels - 1)
    def _():
        up_copy(c).start()

    @pl.when(y == 0)
    def _():
        mate_copy(c).start()

    weights[2].wait()

    def query_step(i, carry):
        part = pl.ds(pl.multiple_of(i * kv_width, kv_width), kv_width)
        out = jnp.dot(normed[...], wq[:, part], preferred_element_type=jnp.float32)
        for h in range(kv_width // HEAD):
            cut = slice(h * HEAD, (h + 1) * HEAD)
            here = pl.ds(pl.multiple_of(i * kv_width + h * HEAD, HEAD), HEAD)
            query[:, here] = rope(out[:, cut]).astype(jnp.bfloat16)
        return carry

    lax.fori_loop(0, group, query_step, 0)

    ones = jnp.ones((rows, HEAD), jnp.bfloat16)

    def attend(b, own):
        for h in range(heads):
            k0 = (h // group) * HEAD
            v0 = kv_width + k0
            expo = expo_of(query[:, h * HEAD : (h + 1) * HEAD], kv[b, :, k0 : k0 + HEAD])
            if own:
                at = lax.broadcasted_iota(jnp.int32, (rows, rows), 0)
                key_at = lax.broadcasted_iota(jnp.int32, (rows, rows), 1)
                expo = jnp.where(key_at <= at, expo, 0.0)
            more = jnp.concatenate([kv[b, :, v0 : v0 + HEAD], ones], axis=1)
            part = jnp.dot(expo.astype(jnp.bfloat16), more, preferred_element_type=jnp.float32)
            if own:
                acc[h] = part
            else:
                acc[h] += part

    attend(c, True)

    def level_step(s, carry):
        level = z - s

        @pl.when(s > 0)
        def _():
            b = 2 * level + y
            up_copy(b).wait_recv()

            @pl.when(z < levels - 1)
            def _():
                up_copy(b).start()

            mate_copy(b).start()
            attend(b, False)

        @pl.when((s > 0) | (y == 1))
        def _():
            b = 2 * level + 1 - y
            mate_copy(b).wait_recv()
            attend(b, False)

        return carry

    lax.fori_loop(0, z + 1, level_step, 0)

    def att_copy(kind, h):
        slot = t if kind < 2 else t_far
        return pltpu.make_async_remote_copy(
            src_ref=att.at[slot, h],
            dst_ref=att.at[slot, h],
            send_sem=att_send.at[kind, h],
            recv_sem=att_recv.at[kind, h],
            device_id=(c, t_far if kind == 0 else t_core),
            device_id_type=MESH,
        )

    for h in range(heads):
        att[t, h] = (acc[h, :, :HEAD] / acc[h, :, HEAD:]).astype(jnp.bfloat16)
        att_copy(0, h).start()
        att_copy(1, h).start()

    for copy in tails:
        copy.wait_recv()

    @pl.when(z == 1)
    def _():
        end_copy(0, False).start()
        end_copy(1, False).start()

    @pl.when(z > 0)
    def _():
        end_copy(0, True).wait_recv()
        end_copy(1, True).wait_recv()

    @pl.when(z < levels - 1)
    def _():
        end_copy(0, True).start()
        end_copy(1, True).start()

    lane = lax.broadcasted_iota(jnp.int32, (rows, HEAD), 1)
    row = lax.broadcasted_iota(jnp.int32, (rows, HEAD), 0) + c * rows
    sink_live = (lane < SINKS) & (lane <= row)
    sinks = jnp.zeros((rows, HEAD), jnp.float32)
    for h in range(heads):
        k0 = (h // group) * HEAD
        sinks += expo_of(query[:, h * HEAD : (h + 1) * HEAD], kv[0, :HEAD, k0 : k0 + HEAD])
    sink_acc[...] = jnp.where(sink_live, sinks, 0.0)

    tile = cols // 3

    def add_slot(slot, first):
        rows_of = jnp.concatenate([att[slot, h] for h in range(heads)], axis=1)
        for i in range(3):
            cut = slice(i * tile, (i + 1) * tile)
            part = jnp.dot(rows_of, wo[slot, :, cut], preferred_element_type=jnp.float32)
            if first:
                proj[:, cut] = part
            else:
                proj[:, cut] += part

    own_wo.wait()
    add_slot(t, True)
    wo_copies[0].wait_recv()
    for h in range(heads):
        att_copy(1, h).wait_recv()
    add_slot(t_core, False)
    for h in range(heads):
        att_copy(0, h).wait_recv()
        att_copy(2, h).start()
    wo_copies[1].wait_recv()

    @pl.when(z == 0)
    def _():
        end_copy(0, False).wait_recv()
        end_copy(1, False).wait_recv()

    add_slot(t_far, False)
    wo_copies[2].wait_recv()
    for h in range(heads):
        att_copy(2, h).wait_recv()
    add_slot(t_diag, False)

    squares = jnp.sum(proj[...] * proj[...], axis=-1, keepdims=True)
    sink_sum = jnp.sum(sink_acc[...], axis=-1, keepdims=True)
    both = jnp.where(lane == 0, squares, sink_sum)
    stat[t] = jnp.transpose(both)[:8, :]

    def stat_copy(i, other):
        return pltpu.make_async_remote_copy(
            src_ref=stat.at[t],
            dst_ref=stat.at[t],
            send_sem=stat_send.at[i],
            recv_sem=stat_recv.at[i],
            device_id=(c, other),
            device_id_type=MESH,
        )

    stats = [stat_copy(i, other) for i, other in enumerate(partners)]
    for copy in stats:
        copy.start()
    for copy in stats:
        copy.wait_recv()
    total = stat[0] + stat[1] + stat[2] + stat[3]
    share_ref[...] = jnp.log(total[1:2, :] / (4.0 * heads))
    column = jnp.transpose(jnp.concatenate([total] * 16, axis=0))[:, :1]
    scale = lax.rsqrt(column / width + 1e-06)
    mine = hid[:, pl.ds(pl.multiple_of(t * cols, 128), cols)].astype(jnp.float32)
    out_ref[...] = (mine + proj[...] * scale * post_ref[...].reshape(1, cols)).astype(jnp.bfloat16)

    @pl.when(z < levels - 1)
    def _():
        up_copy(c).wait_send()
        end_copy(0, True).wait_send()
        end_copy(1, True).wait_send()

    @pl.when(z == 1)
    def _():
        end_copy(0, False).wait_send()
        end_copy(1, False).wait_send()

    @pl.when(y == 0)
    def _():
        mate_copy(c).wait_send()

    def drain_step(s, carry):
        b = 2 * (z - s) + y

        @pl.when(z < levels - 1)
        def _():
            up_copy(b).wait_send()

        mate_copy(b).wait_send()
        return carry

    lax.fori_loop(1, z + 1, drain_step, 0)
    for copy in wo_copies + tails + stats:
        copy.wait_send()
    for kind in range(3):
        for h in range(heads):
            att_copy(kind, h).wait_send()


def fused_on_device(n, hidden_in, pre_gain, w_query, w_key, w_value, w_out, post_gain):
    rows, width = hidden_in.shape
    cols = post_gain.shape[0]
    q_width, kv_width = w_query.shape[1], w_key.shape[1]
    heads = q_width // HEAD
    positions = lax.axis_index("ctx") * rows + jnp.arange(rows, dtype=jnp.int32)
    cosine, sine = rope_tables(positions)
    cosine, sine = cosine[:, 0, :], sine[:, 0, :]
    sine = jnp.where(jnp.arange(HEAD)[None, :] < HEAD // 2, -sine, sine)
    hbm, vmem = pl.BlockSpec(memory_space=pl.ANY), pl.BlockSpec(memory_space=pltpu.VMEM)
    dma = pltpu.SemaphoreType.DMA
    bf16, f32 = jnp.bfloat16, jnp.float32
    layer_out, share = pl.pallas_call(
        functools.partial(fused_kernel, n),
        out_shape=(
            jax.ShapeDtypeStruct((rows, cols), bf16),
            jax.ShapeDtypeStruct((1, rows), f32),
        ),
        in_specs=[hbm] * 5 + [vmem] * 4,
        out_specs=(vmem, vmem),
        scratch_shapes=[
            pltpu.VMEM((rows, width), bf16),
            pltpu.VMEM((rows, width), bf16),
            pltpu.VMEM((width, q_width), bf16),
            pltpu.VMEM((width, kv_width), bf16),
            pltpu.VMEM((width, kv_width), bf16),
            pltpu.VMEM((4, q_width, cols), bf16),
            pltpu.VMEM((rows, q_width), bf16),
            pltpu.VMEM((n, rows, 2 * kv_width), bf16),
            pltpu.VMEM((heads, rows, 2 * HEAD), f32),
            pltpu.VMEM((rows, HEAD), f32),
            pltpu.VMEM((4, heads, rows, HEAD), bf16),
            pltpu.VMEM((rows, cols), f32),
            pltpu.VMEM((4, 8, rows), f32),
            dma((4,)),
            dma((3,)),
            dma,
            dma((3,)),
            dma((3,)),
            dma((n,)),
            dma((n,)),
            dma((n,)),
            dma((2,)),
            dma((2,)),
            dma((2,)),
            dma((2,)),
            dma((2,)),
            dma((3, heads)),
            dma((3, heads)),
            dma((3,)),
            dma((3,)),
        ],
        compiler_params=pltpu.CompilerParams(
            collective_id=0, has_side_effects=True, vmem_limit_bytes=56 * 1024 * 1024
        ),
        cost_estimate=pl.CostEstimate(
            flops=2 * rows * width * (q_width + 2 * kv_width)
            + 4 * rows * n * rows * q_width
            + 8 * rows * q_width * cols,
            bytes_accessed=2 * width * (rows + 2 * q_width + 2 * kv_width),
            transcendentals=2 * heads * rows * n * rows,
        ),
    )(
        hidden_in,
        w_query,
        w_key,
        w_value,
        w_out,
        pre_gain,
        post_gain,
        cosine,
        sine,
    )
    return layer_out, share.reshape(rows)


def solution(mesh):
    n, tp = mesh.shape["ctx"], mesh.shape["tp"]

    def body(*args):
        if n * args[0].shape[0] <= WINDOW and n % 2 == 0 and n >= 4 and tp == 4:
            return fused_on_device(n, *args)
        return on_device(*args)

    return jax.shard_map(
        body,
        mesh=mesh,
        in_specs=(
            P("ctx", None),
            P(),
            P(None, "tp"),
            P(None, "tp"),
            P(None, "tp"),
            P("tp", None),
            P("tp"),
        ),
        out_specs=(P("ctx", "tp"), P("ctx")),
        check_vma=False,
    )
```
